32 devices in a mesh: head: 2 (over y), seq: 16 (over z, x, core).
Axes of the slice: x: 2, y: 2, z: 4, core: 2. Of those that a mesh axis runs over, the one named last changes fastest.
Arguments:
- tokens: bfloat16 [12288, 2048], P('seq', 'head'), may hold values from -6 to 6
- weights: bfloat16 [3, 2048, 2048], P(None, 'seq', 'head'), may hold values from -0.06591797 to 0.06591797
- landmark_pos: int32 [16, 256], P('head'), may hold values from 0 to 12287, as said below
Outputs:
- attended: bfloat16 [12288, 2048], P('seq', 'head')
The draws below stay inside these ranges and needn't reach their ends.
Inputs may be any that keep to these rules, and one draw needn't show every extreme that they name: `landmark_pos`: landmark number j of every head lies in tokens j * 48 to (j + 1) * 48 - 1.
All inputs are finite; a program needn't handle non-finite values. Where the reference program divides by a largest or mean magnitude, that divisor is 1e-20 or more.
Results may differ from the reference program's by a relative error of at most 0.0041.
Values may be sent and summed in bfloat16 or wider, within the bound.
A program may use at most 64 MiB of HBM per device.

```python
import math
import jax
import jax.numpy as jnp
from jax import lax

D = 2048
H = 16
E = 128
M = 256
NSTEPS = 6
SEQ_LEN = 12288


def draw_landmark_pos(key, part):
    offsets = jax.random.randint(key, (H, M), 0, SEQ_LEN // M)
    offsets = offsets.at[0, 0].set(0).at[0, M - 1].set(SEQ_LEN // M - 1)
    starts = jnp.arange(M, dtype=jnp.int32)[None, :] * (SEQ_LEN // M)
    return (starts + offsets).astype(jnp.int32)


def draw_tokens(key, part):
    noise_key = jax.random.fold_in(key, 11)
    block_key = jax.random.fold_in(key, 12)
    noise = jax.random.normal(noise_key, (SEQ_LEN, D), jnp.float32)
    shared = jax.random.normal(block_key, (M, D), jnp.float32)
    whole = noise + jnp.repeat(shared, SEQ_LEN // M, axis=0)
    return jnp.clip(whole, -6.0, 6.0).astype(jnp.bfloat16)


def levels(stream_key, shape, shards, least, top_value):
    gain, own = 1.0, jax.random.fold_in(stream_key, 6)
    for position, blocks in shards:
        draws = jnp.exp(jax.random.uniform(jax.random.fold_in(own, position), (blocks,), jnp.float32, least / len(shards), top_value / len(shards)))
        gain = gain * jnp.repeat(draws, shape[position] // blocks).reshape([-1 if axis == position else 1 for axis in range(len(shape))])
    return gain


def normal_values(stream_key, dims, width, most, pieces=(), kind=jnp.bfloat16):
    values = width * jax.random.normal(stream_key, dims, jnp.float32)
    if pieces:
        values = values * levels(stream_key, dims, pieces, -0.22, 0.18)
    return jnp.clip(values, -most, most).astype(kind)


def setup_inputs(seed: int = 0) -> dict:
    streams_of = jax.random.split(jax.random.key(seed), 4)
    tokens = draw_tokens(jax.random.fold_in(streams_of[3], 71), 0)
    weights = normal_values(streams_of[1], (3, D, H * E), (0.45 * D ** -0.5), 0.06591797, ((1, 16), (2, 2)))
    landmark_pos = draw_landmark_pos(jax.random.fold_in(streams_of[3], 71), 0)
    return {"tokens": tokens, "weights": weights, "landmark_pos": landmark_pos}


def gauss(left, right):
    left32 = left.astype(jnp.float32)
    right32 = right.astype(jnp.float32)
    inner = jnp.einsum('ie,je->ij', left32, right32)
    dist = lax.optimization_barrier(jnp.sum(left32 * left32, -1))[:, None] + lax.optimization_barrier(jnp.sum(right32 * right32, -1))[None, :] - 2.0 * inner
    return jnp.exp(-dist / (2.0 * math.sqrt(left.shape[-1])))

def one_head(packed):
    query, keys, values, places = packed
    even = (jnp.arange(M) % 2 == 0)[:, None]
    landmarks = jnp.where(even, query[places], keys[places])
    inner = gauss(landmarks, landmarks)
    key_weights = gauss(landmarks, keys).astype(jnp.bfloat16)
    summary = jnp.dot(key_weights, values, preferred_element_type=jnp.float32)
    scale_cols = jnp.max(lax.optimization_barrier(jnp.sum(jnp.abs(inner), 0)))
    scale_rows = jnp.max(lax.optimization_barrier(jnp.sum(jnp.abs(inner), 1)))
    iterate = inner / (scale_cols * scale_rows)
    for step in range(NSTEPS):
        left = jnp.dot(iterate, inner, precision=lax.Precision.HIGHEST)
        iterate = 2.0 * iterate - jnp.dot(left, iterate, precision=lax.Precision.HIGHEST)
    mixed = jnp.dot(iterate, summary, precision=lax.Precision.HIGHEST).astype(jnp.bfloat16)
    query_weights = gauss(query, landmarks).astype(jnp.bfloat16)
    return jnp.dot(query_weights, mixed, preferred_element_type=jnp.float32).astype(jnp.bfloat16)

def reference(tokens, weights, landmark_pos):

    def project(index):
        flat = jnp.dot(tokens, weights[index], preferred_element_type=jnp.float32).astype(jnp.bfloat16)
        return jnp.transpose(flat.reshape(SEQ_LEN, H, E), (1, 0, 2))
    query = project(0)
    keys = project(1)
    values = project(2)
    result = lax.map(one_head, (query, keys, values, landmark_pos))
    return jnp.transpose(result, (1, 0, 2)).reshape(SEQ_LEN, H * E)
```

```python
import functools
import math

import jax
import jax.numpy as jnp
from jax import lax
from jax.experimental import pallas as pl
from jax.experimental.pallas import tpu as pltpu
from jax.sharding import PartitionSpec as P

NSTEPS = 6
TILE = 256
CHUNKS = 3
MESH = pl.DeviceIdType.MESH
BF = jnp.bfloat16
F32 = jnp.float32
NT = (((1,), (1,)), ((), ()))


def exact(left, right):
    return jnp.dot(left, right, precision=lax.Precision.HIGHEST, preferred_element_type=F32)


def row_norms(rows):
    wide = rows.astype(F32)
    square = wide * wide
    high = square.astype(BF)
    low = (square - high.astype(F32)).astype(BF)
    ones = jnp.ones((16, rows.shape[1]), BF)
    both = lax.dot_general(ones, high, NT, preferred_element_type=F32) + lax.dot_general(
        ones, low, NT, preferred_element_type=F32
    )
    return both[0:1, :]


def col_norms(rows):
    wide = rows.astype(F32)
    return jnp.sum(wide * wide, -1, keepdims=True)


def gauss(left, right):
    inner = lax.dot_general(left, right, NT, preferred_element_type=F32)
    scale = 1.0 / (2.0 * math.sqrt(left.shape[1]))
    return jnp.exp((2.0 * inner - col_norms(left) - row_norms(right)) * scale)


def kernel(
    n_head, n_seq,
    tok_ref, w_ref, pos_ref, out_ref,
    tokf, wg, acc, qkv, marks, kw, qw, part, parts_in, summ, inv, mixed, obuf,
    loc_sem, wsib_sem, ty_send, ty_recv, ts_send, ts_recv,
    up_send, up_recv, dn_send, dn_recv, x_send, x_recv,
    lm_send, lm_recv, rs_send, rs_recv, ex_send, ex_recv, ag_send, ag_recv,
    os_send, os_recv,
):
    y = lax.axis_index("head")
    s = lax.axis_index("seq")
    core = lax.rem(s, 2)
    chip = s // 2
    x = lax.rem(chip, 2)
    z = s // 4
    nz = n_seq // 4
    nch = n_seq // 2
    toks, feats = tok_ref.shape
    rows, half = w_ref.shape[1], w_ref.shape[2] // 2
    heads = pos_ref.shape[0]
    per_chip = pos_ref.shape[1]
    size = half // heads
    marks_n = per_chip * nch
    group = nch // heads
    share = marks_n // group
    sib = (y, s + 1 - 2 * core)
    xpeer = (y, s + 2 - 4 * x)
    waits = []

    def remote(src, dst, send, recv, device):
        return pltpu.make_async_remote_copy(
            src_ref=src, dst_ref=dst, send_sem=send, recv_sem=recv,
            device_id=device, device_id_type=MESH,
        )

    def chip_dev(offset):
        return (y, lax.rem(chip + offset, nch) * 2 + core)

    def head_dev(offset):
        return (lax.rem(y + offset, n_head), s)

    barrier = pltpu.get_barrier_semaphore()
    peers = [sib] + [head_dev(i) for i in range(1, n_head)] + [chip_dev(i) for i in range(1, nch)]
    for peer in peers:
        pl.semaphore_signal(barrier, inc=1, device_id=peer, device_id_type=MESH)
    pl.semaphore_wait(barrier, len(peers))

    def my_rows(seq_index):
        return pl.ds(pl.multiple_of(seq_index * rows, rows), rows)

    def half_cols(which):
        return pl.ds(pl.multiple_of(which * half, half), half)

    wsib = remote(
        w_ref.at[:, :, half_cols(1 - core)], wg.at[:, my_rows(s), :], wsib_sem.at[0],
        wsib_sem.at[1], sib,
    )
    wsib.start()
    wloc = pltpu.make_async_copy(
        w_ref.at[:, :, half_cols(core)], wg.at[:, my_rows(s), :], loc_sem.at[0]
    )
    wloc.start()
    chunk = toks // CHUNKS

    def tok_block(owner, part_index, which_core=None):
        which = core if which_core is None else which_core
        return tokf.at[
            pl.ds(pl.multiple_of(which * toks + part_index * chunk, chunk), chunk),
            pl.ds(pl.multiple_of(owner * feats, feats), feats),
        ]

    def tok_own(part_index):
        return tok_ref.at[pl.ds(part_index * chunk, chunk), :]

    for k in range(CHUNKS):
        for i in range(1, n_head):
            copy = remote(
                tok_own(k), tok_block(y, k), ty_send.at[i, k], ty_recv.at[i, k], head_dev(i)
            )
            copy.start()
            waits.append((None, copy))
    tloc = pltpu.make_async_copy(
        tok_ref,
        tokf.at[
            pl.ds(pl.multiple_of(core * toks, toks), toks),
            pl.ds(pl.multiple_of(y * feats, feats), feats),
        ],
        loc_sem.at[1],
    )
    tloc.start()
    wloc.wait()
    wsib.wait()

    for k in range(CHUNKS):
        copy = remote(tok_own(k), tok_block(y, k), ts_send.at[0, k], ts_recv.at[0, k], sib)
        copy.start()
        waits.append((None, copy))

    def block(phase, zb, xb):
        which = pl.ds(0, 2) if phase == 0 else pl.ds(2, 1)
        at = pl.multiple_of((zb * 2 + xb) * 2 * rows, 2 * rows)
        return wg.at[which, pl.ds(at, 2 * rows), :]

    def guarded(condition, copy_of):
        @pl.when(condition)
        def _():
            copy_of().start()

        waits.append((condition, copy_of))

    def up(phase, t):
        def copy():
            ref = block(phase, z - t, x)
            return remote(ref, ref, up_send.at[phase, t], up_recv.at[phase, t], (y, s + 4))

        return copy

    def down(phase, t):
        def copy():
            ref = block(phase, z + t, x)
            return remote(ref, ref, dn_send.at[phase, t], dn_recv.at[phase, t], (y, s - 4))

        return copy

    def across(phase, zb):
        def copy():
            ref = block(phase, zb, x)
            return remote(ref, ref, x_send.at[phase, zb], x_recv.at[phase, zb], xpeer)

        return copy

    def from_below(phase, t):
        ref = block(phase, z - 1 - t, x)
        return remote(ref, ref, up_send.at[phase, t], up_recv.at[phase, t], (y, s - 4))

    def from_above(phase, t):
        ref = block(phase, z + 1 + t, x)
        return remote(ref, ref, dn_send.at[phase, t], dn_recv.at[phase, t], (y, s + 4))

    def line_start(phase):
        guarded(z + 1 < nz, up(phase, 0))
        guarded(z >= 1, down(phase, 0))
        copy = across(phase, z)()
        copy.start()
        waits.append((None, copy))

    def line_step(phase, t):
        below = z - 1 - t >= 0
        above = z + 1 + t < nz

        @pl.when(below)
        def _():
            from_below(phase, t).wait_recv()

        if t + 1 < nz - 1:
            guarded(below & (z + 1 < nz), up(phase, t + 1))
        guarded(below, across(phase, z - 1 - t))

        @pl.when(above)
        def _():
            from_above(phase, t).wait_recv()

        if t + 1 < nz - 1:
            guarded(above & (z >= 1), down(phase, t + 1))
        guarded(above, across(phase, z + 1 + t))

    def across_wait(phase, zb):
        ref = block(phase, zb, 1 - x)
        remote(ref, ref, x_send.at[phase, zb], x_recv.at[phase, zb], xpeer).wait_recv()

    def forward_tokens(k):
        for i in range(1, n_head):
            owner = lax.rem(y + n_head - i, n_head)
            ref = tok_block(owner, k)
            remote(ref, ref, ty_send.at[i, k], ty_recv.at[i, k], head_dev(n_head - i)).wait_recv()
            copy = remote(ref, ref, ts_send.at[i, k], ts_recv.at[i, k], sib)
            copy.start()
            waits.append((None, copy))

    line_start(0)
    for t in range(nz - 1):
        line_step(0, t)
        if t < CHUNKS:
            forward_tokens(t)
    for k in range(nz - 1, CHUNKS):
        forward_tokens(k)
    line_start(1)
    tloc.wait()
    for i in range(n_head):
        owner = lax.rem(y + n_head - i, n_head)
        for k in range(CHUNKS):
            ref = tok_block(owner, k, 1 - core)
            remote(ref, ref, ts_send.at[i, k], ts_recv.at[i, k], sib).wait_recv()

    order = [jnp.where(z < nz // 2, i, nz - 1 - i) for i in range(nz)]
    near, far = order[: nz - nz // 4], order[nz - nz // 4 :]
    deep = 4 * rows

    def project(p, blocks, last):
        def body(i, carry):
            at = pl.ds(pl.multiple_of(i * TILE, TILE), TILE)
            total = None
            for zb in blocks:
                inner = pl.ds(pl.multiple_of(zb * deep, deep), deep)
                term = jnp.dot(tokf[at, inner], wg[p, inner, :], preferred_element_type=F32)
                total = term if total is None else total + term
            if last:
                qkv[p, at, :] = (acc[p, at, :] + total).astype(BF)
            else:
                acc[p, at, :] = total
            return carry

        lax.fori_loop(0, 2 * toks // TILE, body, 0)

    for zb in near:
        across_wait(0, zb)
    project(0, near, False)
    line_step(1, 0)
    project(1, near, False)
    for zb in far:
        across_wait(0, zb)
    project(0, far, True)
    project(1, far, True)
    for t in range(1, nz - 1):
        line_step(1, t)

    def cols(h):
        return pl.ds(h * size, size)

    places = lax.broadcasted_iota(jnp.int32, (per_chip, 2 * toks), 1)
    even = lax.broadcasted_iota(jnp.int32, (per_chip, size), 0) % 2 == 0
    for h in range(heads):
        picker = jnp.where(places == pos_ref[h], 1.0, 0.0).astype(BF)
        picked_q = jnp.dot(picker, qkv[0, :, cols(h)], preferred_element_type=F32)
        picked_k = jnp.dot(picker, qkv[1, :, cols(h)], preferred_element_type=F32)
        marks[chip, h] = jnp.where(even, picked_q, picked_k).astype(BF)

    def all_chips(source, buffer, send, recv, index=lambda offset: chip):
        for i in range(1, nch):
            copy = remote(source(i), buffer, send.at[i], recv.at[i], chip_dev(i))
            copy.start()
            waits.append((None, copy))

    def from_chips(buffer, send, recv):
        for i in range(1, nch):
            ref = buffer.at[lax.rem(chip + nch - i, nch)]
            remote(ref, ref, send.at[i], recv.at[i], chip_dev(nch - i)).wait_recv()

    all_chips(lambda i: marks.at[chip], marks.at[chip], lm_send, lm_recv)
    from_chips(marks, lm_send, lm_recv)

    def marks_of(h):
        return marks[:, h].astype(F32).reshape(marks_n, size).astype(BF)

    for h in range(heads):
        own = marks_of(h)

        def weigh(i, carry):
            at = pl.ds(pl.multiple_of(i * TILE, TILE), TILE)
            kw[h, :, at] = gauss(own, qkv[1, at, cols(h)]).astype(BF)
            return carry

        lax.fori_loop(0, 2 * toks // TILE, weigh, 0)

    mine = marks_of(chip // group)
    inner = gauss(mine, mine)
    scale_cols = jnp.max(jnp.sum(jnp.abs(inner), 0, keepdims=True))
    scale_rows = jnp.max(jnp.sum(jnp.abs(inner), 1, keepdims=True))
    iterate = inner / (scale_cols * scale_rows)
    for step in range(NSTEPS):
        iterate = 2.0 * iterate - exact(exact(iterate, inner), iterate)
    inv[...] = iterate

    for zb in near:
        across_wait(1, zb)
    project(2, near, False)
    for zb in far:
        across_wait(1, zb)
    project(2, far, True)

    for h in range(heads):
        total = jnp.dot(kw[h], qkv[2, :, cols(h)], preferred_element_type=F32)
        for j in range(group):
            part[h * group + j] = total[j * share : (j + 1) * share]
    all_chips(
        lambda i: part.at[lax.rem(chip + i, nch)], parts_in.at[chip], rs_send, rs_recv
    )
    for h in range(heads):
        own = marks_of(h)

        def weigh_q(i, carry):
            at = pl.ds(pl.multiple_of(i * TILE, TILE), TILE)
            qw[h, at, :] = gauss(qkv[0, at, cols(h)], own).astype(BF)
            return carry

        lax.fori_loop(0, 2 * toks // TILE, weigh_q, 0)
    from_chips(parts_in, rs_send, rs_recv)
    total = part[chip]
    for i in range(1, nch):
        total = total + parts_in[lax.rem(chip + i, nch)]
    member = lax.rem(chip, group)
    base = chip - member
    summ[member] = total

    def mate(i):
        return lax.rem(member + i, group)

    for i in range(1, group):
        ref = summ.at[member]
        copy = remote(ref, ref, ex_send.at[i], ex_recv.at[i], (y, (base + mate(i)) * 2 + core))
        copy.start()
        waits.append((None, copy))
    for i in range(1, group):
        source = mate(group - i)
        ref = summ.at[source]
        remote(ref, ref, ex_send.at[i], ex_recv.at[i], (y, (base + source) * 2 + core)).wait_recv()
    some = inv[pl.ds(pl.multiple_of(member * share, share), share), :]
    mixed[chip] = exact(some, summ[...].reshape(marks_n, size)).astype(BF)
    all_chips(lambda i: mixed.at[chip], mixed.at[chip], ag_send, ag_recv)
    from_chips(mixed, ag_send, ag_recv)

    own_at = pl.ds(pl.multiple_of(core * toks, toks), toks)
    sib_at = pl.ds(pl.multiple_of((1 - core) * toks, toks), toks)
    for h in range(heads):
        values = jnp.concatenate(
            [mixed[h * group + j].astype(F32) for j in range(group)], axis=0
        ).astype(BF)
        obuf[h] = jnp.dot(qw[h, sib_at, :], values, preferred_element_type=F32).astype(BF)
        where = pl.ds(pl.multiple_of(core * half + h * size, size), size)
        copy = remote(obuf.at[h], out_ref.at[:, where], os_send.at[h], os_recv.at[h], sib)
        copy.start()
        waits.append((None, copy))
        out_ref[:, where] = jnp.dot(
            qw[h, own_at, :], values, preferred_element_type=F32
        ).astype(BF)
    for h in range(heads):
        where = pl.ds(pl.multiple_of((1 - core) * half + h * size, size), size)
        remote(obuf.at[h], out_ref.at[:, where], os_send.at[h], os_recv.at[h], sib).wait_recv()

    for condition, copy in waits:
        if condition is None:
            copy.wait_send()
        else:
            pl.when(condition)(lambda: copy().wait_send())


def shards(tokens, weights, landmark_pos, n_head, n_seq):
    toks, feats = tokens.shape
    _, rows, wide = weights.shape
    heads = landmark_pos.shape[0] // 2
    marks_n = landmark_pos.shape[1]
    half = wide // 2
    size = half // heads
    nch, nz = n_seq // 2, n_seq // 4
    per_chip = marks_n // nch
    group = nch // heads
    share = marks_n // group
    s = lax.axis_index("seq")
    chip, core = s // 2, lax.rem(s, 2)
    pos = lax.dynamic_slice(landmark_pos, (core * heads, chip * per_chip), (heads, per_chip))
    pos = (pos - chip * (2 * toks))[:, :, None]
    dma = pltpu.SemaphoreType.DMA
    vmem = pl.BlockSpec(memory_space=pltpu.VMEM)
    return pl.pallas_call(
        functools.partial(kernel, n_head, n_seq),
        out_shape=jax.ShapeDtypeStruct((toks, wide), BF),
        in_specs=[vmem] * 3,
        out_specs=vmem,
        scratch_shapes=[
            pltpu.VMEM((2 * toks, n_head * feats), BF),
            pltpu.VMEM((3, n_seq * rows, half), BF),
            pltpu.VMEM((3, 2 * toks, half), F32),
            pltpu.VMEM((3, 2 * toks, half), BF),
            pltpu.VMEM((nch, heads, per_chip, size), BF),
            pltpu.VMEM((heads, marks_n, 2 * toks), BF),
            pltpu.VMEM((heads, 2 * toks, marks_n), BF),
            pltpu.VMEM((nch, share, size), F32),
            pltpu.VMEM((nch, share, size), F32),
            pltpu.VMEM((group, share, size), F32),
            pltpu.VMEM((marks_n, marks_n), F32),
            pltpu.VMEM((nch, share, size), BF),
            pltpu.VMEM((heads, toks, size), BF),
            dma((2,)), dma((2,)),
            dma((n_head, CHUNKS)), dma((n_head, CHUNKS)),
            dma((n_head, CHUNKS)), dma((n_head, CHUNKS)),
            dma((2, nz - 1)), dma((2, nz - 1)), dma((2, nz - 1)), dma((2, nz - 1)),
            dma((2, nz)), dma((2, nz)),
            dma((nch,)), dma((nch,)), dma((nch,)), dma((nch,)),
            dma((group,)), dma((group,)), dma((nch,)), dma((nch,)),
            dma((heads,)), dma((heads,)),
        ],
        compiler_params=pltpu.CompilerParams(
            collective_id=0, has_side_effects=True, vmem_limit_bytes=56 * 2**20
        ),
    )(tokens, weights, pos)


def solution(mesh):
    return jax.shard_map(
        functools.partial(shards, n_head=mesh.shape["head"], n_seq=mesh.shape["seq"]),
        mesh=mesh,
        in_specs=(P("seq", "head"), P(None, "seq", "head"), P("head", None)),
        out_specs=P("seq", "head"),
        check_vma=False,
    )
```

```python
import functools
import math

import jax
import jax.numpy as jnp
from jax import lax
from jax.experimental import pallas as pl
from jax.experimental.pallas import tpu as pltpu
from jax.sharding import PartitionSpec as P

NSTEPS = 6
TILE = 256
CHUNKS = 3
MESH = pl.DeviceIdType.MESH
BF = jnp.bfloat16
F32 = jnp.float32
NT = (((1,), (1,)), ((), ()))


def exact(left, right):
    return jnp.dot(left, right, precision=lax.Precision.HIGHEST, preferred_element_type=F32)


def row_norms(rows):
    wide = rows.astype(F32)
    square = wide * wide
    high = square.astype(BF)
    low = (square - high.astype(F32)).astype(BF)
    ones = jnp.ones((16, rows.shape[1]), BF)
    both = lax.dot_general(ones, high, NT, preferred_element_type=F32) + lax.dot_general(
        ones, low, NT, preferred_element_type=F32
    )
    return both[0:1, :]


def col_norms(rows):
    wide = rows.astype(F32)
    return jnp.sum(wide * wide, -1, keepdims=True)


def gauss(left, right):
    inner = lax.dot_general(left, right, NT, preferred_element_type=F32)
    scale = 1.0 / (2.0 * math.sqrt(left.shape[1]))
    return jnp.exp((2.0 * inner - col_norms(left) - row_norms(right)) * scale)


def kernel(
    n_head, n_seq,
    tok_ref, w_ref, pos_ref, out_ref,
    tokf, wg, acc, qkv, marks, kw, qw, part, parts_in, summ, inv, mixed, obuf,
    loc_sem, wsib_sem, ty_send, ty_recv, ts_send, ts_recv,
    up_send, up_recv, dn_send, dn_recv, x_send, x_recv, near_send, near_recv,
    lm_send, lm_recv, rs_send, rs_recv, ex_send, ex_recv, ag_send, ag_recv,
    os_send, os_recv,
):
    y = lax.axis_index("head")
    s = lax.axis_index("seq")
    core = lax.rem(s, 2)
    chip = s // 2
    x = lax.rem(chip, 2)
    z = s // 4
    nz = n_seq // 4
    nch = n_seq // 2
    toks, feats = tok_ref.shape
    rows, half = w_ref.shape[1], w_ref.shape[2] // 2
    heads, marks_n = pos_ref.shape[0] // 2, pos_ref.shape[1]
    per_chip = marks_n // nch
    size = half // heads
    group = nch // heads
    share = marks_n // group
    sib = (y, s + 1 - 2 * core)
    xpeer = (y, s + 2 - 4 * x)
    waits = []

    def remote(src, dst, send, recv, device):
        return pltpu.make_async_remote_copy(
            src_ref=src, dst_ref=dst, send_sem=send, recv_sem=recv,
            device_id=device, device_id_type=MESH,
        )

    def chip_dev(offset):
        return (y, lax.rem(chip + offset, nch) * 2 + core)

    def head_dev(offset):
        return (lax.rem(y + offset, n_head), s)

    barrier = pltpu.get_barrier_semaphore()
    peers = [sib] + [head_dev(i) for i in range(1, n_head)] + [chip_dev(i) for i in range(1, nch)]
    for peer in peers:
        pl.semaphore_signal(barrier, inc=1, device_id=peer, device_id_type=MESH)
    pl.semaphore_wait(barrier, len(peers))

    def my_rows(seq_index):
        return pl.ds(pl.multiple_of(seq_index * rows, rows), rows)

    def half_cols(which):
        return pl.ds(pl.multiple_of(which * half, half), half)

    wsib = remote(
        w_ref.at[:, :, half_cols(1 - core)], wg.at[:, my_rows(s), :], wsib_sem.at[0],
        wsib_sem.at[1], sib,
    )
    wsib.start()
    wloc = pltpu.make_async_copy(
        w_ref.at[:, :, half_cols(core)], wg.at[:, my_rows(s), :], loc_sem.at[0]
    )
    wloc.start()
    chunk = toks // CHUNKS

    def tok_block(owner, part_index, which_core=None):
        which = core if which_core is None else which_core
        return tokf.at[
            pl.ds(pl.multiple_of(which * toks + part_index * chunk, chunk), chunk),
            pl.ds(pl.multiple_of(owner * feats, feats), feats),
        ]

    def tok_own(part_index):
        return tok_ref.at[pl.ds(part_index * chunk, chunk), :]

    for k in range(CHUNKS):
        for i in range(1, n_head):
            copy = remote(
                tok_own(k), tok_block(y, k), ty_send.at[i, k], ty_recv.at[i, k], head_dev(i)
            )
            copy.start()
            waits.append((None, copy))
    tloc = pltpu.make_async_copy(
        tok_ref,
        tokf.at[
            pl.ds(pl.multiple_of(core * toks, toks), toks),
            pl.ds(pl.multiple_of(y * feats, feats), feats),
        ],
        loc_sem.at[1],
    )
    tloc.start()
    wloc.wait()
    wsib.wait()

    for k in range(CHUNKS):
        copy = remote(tok_own(k), tok_block(y, k), ts_send.at[0, k], ts_recv.at[0, k], sib)
        copy.start()
        waits.append((None, copy))

    def block(phase, zb, xb):
        at = pl.multiple_of((zb * 2 + xb) * 2 * rows, 2 * rows)
        return wg.at[phase, pl.ds(at, 2 * rows), :]

    def guarded(condition, copy_of):
        @pl.when(condition)
        def _():
            copy_of().start()

        waits.append((condition, copy_of))

    def up(phase, t):
        def copy():
            ref = block(phase, z - t, x)
            return remote(ref, ref, up_send.at[phase, t], up_recv.at[phase, t], (y, s + 4))

        return copy

    def down(phase, t):
        def copy():
            ref = block(phase, z + t, x)
            return remote(ref, ref, dn_send.at[phase, t], dn_recv.at[phase, t], (y, s - 4))

        return copy

    def across(phase, zb):
        def copy():
            ref = block(phase, zb, x)
            return remote(ref, ref, x_send.at[phase, zb], x_recv.at[phase, zb], xpeer)

        return copy

    def from_below(phase, t):
        ref = block(phase, z - 1 - t, x)
        return remote(ref, ref, up_send.at[phase, t], up_recv.at[phase, t], (y, s - 4))

    def from_above(phase, t):
        ref = block(phase, z + 1 + t, x)
        return remote(ref, ref, dn_send.at[phase, t], dn_recv.at[phase, t], (y, s + 4))

    def line_start(phase):
        guarded(z + 1 < nz, up(phase, 0))
        guarded(z >= 1, down(phase, 0))
        copy = across(phase, z)()
        copy.start()
        waits.append((None, copy))

    def line_step(phase, t):
        below = z - 1 - t >= 0
        above = z + 1 + t < nz

        @pl.when(below)
        def _():
            from_below(phase, t).wait_recv()

        if t + 1 < nz - 1:
            guarded(below & (z + 1 < nz), up(phase, t + 1))
        if phase < 2 or t > 0:
            guarded(below, across(phase, z - 1 - t))

        @pl.when(above)
        def _():
            from_above(phase, t).wait_recv()

        if t + 1 < nz - 1:
            guarded(above & (z >= 1), down(phase, t + 1))
        if phase < 2 or t > 0:
            guarded(above, across(phase, z + 1 + t))

    def across_wait(phase, zb):
        ref = block(phase, zb, 1 - x)
        remote(ref, ref, x_send.at[phase, zb], x_recv.at[phase, zb], xpeer).wait_recv()

    def forward_tokens(k):
        for i in range(1, n_head):
            owner = lax.rem(y + n_head - i, n_head)
            ref = tok_block(owner, k)
            remote(ref, ref, ty_send.at[i, k], ty_recv.at[i, k], head_dev(n_head - i)).wait_recv()
            copy = remote(ref, ref, ts_send.at[i, k], ts_recv.at[i, k], sib)
            copy.start()
            waits.append((None, copy))

    line_start(0)
    line_start(1)
    for t in range(nz - 1):
        line_step(0, t)
        line_step(1, t)
        if t < CHUNKS:
            forward_tokens(t)
    for k in range(nz - 1, CHUNKS):
        forward_tokens(k)
    line_start(2)
    tloc.wait()
    for i in range(n_head):
        owner = lax.rem(y + n_head - i, n_head)
        for k in range(CHUNKS):
            ref = tok_block(owner, k, 1 - core)
            remote(ref, ref, ts_send.at[i, k], ts_recv.at[i, k], sib).wait_recv()

    order = [jnp.where(z < nz // 2, i, nz - 1 - i) for i in range(nz)]
    near, far = order[: nz - nz // 4], order[nz - nz // 4 :]
    deep = 4 * rows

    def project(p, blocks, last):
        def body(i, carry):
            at = pl.ds(pl.multiple_of(i * TILE, TILE), TILE)
            total = None
            for zb in blocks:
                inner = pl.ds(pl.multiple_of(zb * deep, deep), deep)
                term = jnp.dot(tokf[at, inner], wg[p, inner, :], preferred_element_type=F32)
                total = term if total is None else total + term
            if last:
                qkv[p, at, :] = (acc[p, at, :] + total).astype(BF)
            else:
                acc[p, at, :] = total
            return carry

        lax.fori_loop(0, 2 * toks // TILE, body, 0)

    def neighbour(step, plane):
        ref = block(2, plane, 1 - x)
        way = (step + 1) // 2
        return remote(ref, ref, near_send.at[way], near_recv.at[way], (y, s + 4 * step))

    def values_wait(zb):
        pl.when(zb == z - 1)(lambda: neighbour(1, z - 1).wait_recv())
        pl.when(zb == z + 1)(lambda: neighbour(-1, z + 1).wait_recv())
        pl.when((zb < z - 1) | (zb > z + 1))(lambda: across_wait(2, zb))

    for zb in near:
        across_wait(0, zb)
    project(0, near, False)
    line_step(2, 0)
    for zb in near:
        across_wait(1, zb)
    project(1, near, False)
    for t in range(1, nz - 1):
        line_step(2, t)
    for zb in far:
        across_wait(0, zb)
    project(0, far, True)
    for zb in far:
        across_wait(1, zb)
    project(1, far, True)

    def cols(h):
        return pl.ds(h * size, size)

    places = lax.broadcasted_iota(jnp.int32, (per_chip, 2 * toks), 1)
    even = lax.broadcasted_iota(jnp.int32, (per_chip, size), 0) % 2 == 0
    own_mark = lax.broadcasted_iota(jnp.int32, (per_chip, marks_n), 1) == (
        chip * per_chip + lax.broadcasted_iota(jnp.int32, (per_chip, marks_n), 0)
    )
    first = chip * (2 * toks)
    for h in range(heads):
        head_pos = pos_ref[pl.ds(core * heads + h, 1), :]
        place = jnp.sum(jnp.where(own_mark, head_pos, 0), -1, keepdims=True) - first
        picker = jnp.where(places == place, 1.0, 0.0).astype(BF)
        picked_q = jnp.dot(picker, qkv[0, :, cols(h)], preferred_element_type=F32)
        picked_k = jnp.dot(picker, qkv[1, :, cols(h)], preferred_element_type=F32)
        marks[chip, h] = jnp.where(even, picked_q, picked_k).astype(BF)

    def all_chips(source, buffer, send, recv):
        for i in range(1, nch):
            copy = remote(source(i), buffer, send.at[i], recv.at[i], chip_dev(i))
            copy.start()
            waits.append((None, copy))

    def from_chips(buffer, send, recv):
        for i in range(1, nch):
            ref = buffer.at[lax.rem(chip + nch - i, nch)]
            remote(ref, ref, send.at[i], recv.at[i], chip_dev(nch - i)).wait_recv()

    all_chips(lambda i: marks.at[chip], marks.at[chip], lm_send, lm_recv)
    across_wait(2, z)
    guarded(z + 1 < nz, lambda: neighbour(1, z))
    guarded(z >= 1, lambda: neighbour(-1, z))
    for zb in near:
        values_wait(zb)
    project(2, near, False)
    from_chips(marks, lm_send, lm_recv)

    def marks_of(h):
        return marks[:, h].astype(F32).reshape(marks_n, size).astype(BF)

    for h in range(heads):
        own = marks_of(h)

        def weigh(i, carry):
            at = pl.ds(pl.multiple_of(i * TILE, TILE), TILE)
            kw[h, :, at] = gauss(own, qkv[1, at, cols(h)]).astype(BF)
            return carry

        lax.fori_loop(0, 2 * toks // TILE, weigh, 0)

    for zb in far:
        values_wait(zb)
    project(2, far, True)

    for h in range(heads):
        total = jnp.dot(kw[h], qkv[2, :, cols(h)], preferred_element_type=F32)
        for j in range(group):
            part[h * group + j] = total[j * share : (j + 1) * share]
    all_chips(
        lambda i: part.at[lax.rem(chip + i, nch)], parts_in.at[chip], rs_send, rs_recv
    )
    mine = marks_of(chip // group)
    inner = gauss(mine, mine)
    scale_cols = jnp.max(jnp.sum(jnp.abs(inner), 0, keepdims=True))
    scale_rows = jnp.max(jnp.sum(jnp.abs(inner), 1, keepdims=True))
    iterate = inner / (scale_cols * scale_rows)
    for step in range(NSTEPS):
        iterate = 2.0 * iterate - exact(exact(iterate, inner), iterate)
    inv[...] = iterate

    for h in range(heads):
        own = marks_of(h)

        def weigh_q(i, carry):
            at = pl.ds(pl.multiple_of(i * TILE, TILE), TILE)
            qw[h, at, :] = gauss(qkv[0, at, cols(h)], own).astype(BF)
            return carry

        lax.fori_loop(0, 2 * toks // TILE, weigh_q, 0)
    from_chips(parts_in, rs_send, rs_recv)
    total = part[chip]
    for i in range(1, nch):
        total = total + parts_in[lax.rem(chip + i, nch)]
    member = lax.rem(chip, group)
    base = chip - member
    summ[member] = total

    def mate(i):
        return lax.rem(member + i, group)

    for i in range(1, group):
        ref = summ.at[member]
        copy = remote(ref, ref, ex_send.at[i], ex_recv.at[i], (y, (base + mate(i)) * 2 + core))
        copy.start()
        waits.append((None, copy))
    for i in range(1, group):
        source = mate(group - i)
        ref = summ.at[source]
        remote(ref, ref, ex_send.at[i], ex_recv.at[i], (y, (base + source) * 2 + core)).wait_recv()
    owned = chip // group
    mixed[owned] = exact(inv[...], summ[...].reshape(marks_n, size)).astype(BF)

    def like(offset):
        return (y, (lax.rem(owned + offset, heads) * group + member) * 2 + core)

    for i in range(1, heads):
        ref = mixed.at[owned]
        copy = remote(ref, ref, ag_send.at[i], ag_recv.at[i], like(i))
        copy.start()
        waits.append((None, copy))
    for i in range(1, heads):
        ref = mixed.at[lax.rem(owned + heads - i, heads)]
        remote(ref, ref, ag_send.at[i], ag_recv.at[i], like(heads - i)).wait_recv()

    own_at = pl.ds(pl.multiple_of(core * toks, toks), toks)
    sib_at = pl.ds(pl.multiple_of((1 - core) * toks, toks), toks)
    for h in range(heads):
        values = mixed[h]
        obuf[h] = jnp.dot(qw[h, sib_at, :], values, preferred_element_type=F32).astype(BF)
        where = pl.ds(pl.multiple_of(core * half + h * size, size), size)
        copy = remote(obuf.at[h], out_ref.at[:, where], os_send.at[h], os_recv.at[h], sib)
        copy.start()
        waits.append((None, copy))
        out_ref[:, where] = jnp.dot(
            qw[h, own_at, :], values, preferred_element_type=F32
        ).astype(BF)
    for h in range(heads):
        where = pl.ds(pl.multiple_of((1 - core) * half + h * size, size), size)
        remote(obuf.at[h], out_ref.at[:, where], os_send.at[h], os_recv.at[h], sib).wait_recv()

    for condition, copy in waits:
        if condition is None:
            copy.wait_send()
        else:
            pl.when(condition)(lambda: copy().wait_send())


def shards(tokens, weights, landmark_pos, n_head, n_seq):
    toks, feats = tokens.shape
    _, rows, wide = weights.shape
    heads = landmark_pos.shape[0] // 2
    marks_n = landmark_pos.shape[1]
    half = wide // 2
    size = half // heads
    nch, nz = n_seq // 2, n_seq // 4
    per_chip = marks_n // nch
    group = nch // heads
    share = marks_n // group
    dma = pltpu.SemaphoreType.DMA
    vmem = pl.BlockSpec(memory_space=pltpu.VMEM)
    return pl.pallas_call(
        functools.partial(kernel, n_head, n_seq),
        out_shape=jax.ShapeDtypeStruct((toks, wide), BF),
        in_specs=[vmem] * 3,
        out_specs=vmem,
        scratch_shapes=[
            pltpu.VMEM((2 * toks, n_head * feats), BF),
            pltpu.VMEM((3, n_seq * rows, half), BF),
            pltpu.VMEM((3, 2 * toks, half), F32),
            pltpu.VMEM((3, 2 * toks, half), BF),
            pltpu.VMEM((nch, heads, per_chip, size), BF),
            pltpu.VMEM((heads, marks_n, 2 * toks), BF),
            pltpu.VMEM((heads, 2 * toks, marks_n), BF),
            pltpu.VMEM((nch, share, size), F32),
            pltpu.VMEM((nch, share, size), F32),
            pltpu.VMEM((group, share, size), F32),
            pltpu.VMEM((marks_n, marks_n), F32),
            pltpu.VMEM((heads, marks_n, size), BF),
            pltpu.VMEM((heads, toks, size), BF),
            dma((2,)), dma((2,)),
            dma((n_head, CHUNKS)), dma((n_head, CHUNKS)),
            dma((n_head, CHUNKS)), dma((n_head, CHUNKS)),
            dma((3, nz - 1)), dma((3, nz - 1)), dma((3, nz - 1)), dma((3, nz - 1)),
            dma((3, nz)), dma((3, nz)), dma((2,)), dma((2,)),
            dma((nch,)), dma((nch,)), dma((nch,)), dma((nch,)),
            dma((group,)), dma((group,)), dma((heads,)), dma((heads,)),
            dma((heads,)), dma((heads,)),
        ],
        compiler_params=pltpu.CompilerParams(
            collective_id=0, has_side_effects=True, vmem_limit_bytes=56 * 2**20
        ),
    )(tokens, weights, landmark_pos)


def solution(mesh):
    return jax.shard_map(
        functools.partial(shards, n_head=mesh.shape["head"], n_seq=mesh.shape["seq"]),
        mesh=mesh,
        in_specs=(P("seq", "head"), P(None, "seq", "head"), P("head", None)),
        out_specs=P("seq", "head"),
        check_vma=False,
    )
```

```python
import functools
import math

import jax
import jax.numpy as jnp
from jax import lax
from jax.experimental import pallas as pl
from jax.experimental.pallas import tpu as pltpu
from jax.sharding import PartitionSpec as P

NSTEPS = 6
TILE = 256
CHUNKS = 3
MESH = pl.DeviceIdType.MESH
BF = jnp.bfloat16
F32 = jnp.float32
NT = (((1,), (1,)), ((), ()))


def exact(left, right):
    return jnp.dot(left, right, precision=lax.Precision.HIGHEST, preferred_element_type=F32)


def row_norms(rows):
    wide = rows.astype(F32)
    square = wide * wide
    high = square.astype(BF)
    low = (square - high.astype(F32)).astype(BF)
    ones = jnp.ones((16, rows.shape[1]), BF)
    both = lax.dot_general(ones, high, NT, preferred_element_type=F32) + lax.dot_general(
        ones, low, NT, preferred_element_type=F32
    )
    return both[0:1, :]


def col_norms(rows):
    wide = rows.astype(F32)
    return jnp.sum(wide * wide, -1, keepdims=True)


def gauss(left, right):
    inner = lax.dot_general(left, right, NT, preferred_element_type=F32)
    scale = 1.0 / (2.0 * math.sqrt(left.shape[1]))
    return jnp.exp((2.0 * inner - col_norms(left) - row_norms(right)) * scale)


def kernel(
    n_head, n_seq,
    tok_ref, w_ref, pos_ref, out_ref,
    tokf, wg, acc, qkv, marks, kw, qw, part, parts_in, summ, inv, mixed, obuf,
    loc_sem, wsib_sem, ty_send, ty_recv, ts_send, ts_recv,
    up_send, up_recv, dn_send, dn_recv, x_send, x_recv, near_send, near_recv,
    lm_send, lm_recv, rs_send, rs_recv, ex_send, ex_recv, ag_send, ag_recv,
    os_send, os_recv,
):
    y = lax.axis_index("head")
    s = lax.axis_index("seq")
    core = lax.rem(s, 2)
    chip = s // 2
    x = lax.rem(chip, 2)
    z = s // 4
    nz = n_seq // 4
    nch = n_seq // 2
    toks, feats = tok_ref.shape
    rows, half = w_ref.shape[1], w_ref.shape[2] // 2
    heads, marks_n = pos_ref.shape[0] // 2, pos_ref.shape[1]
    per_chip = marks_n // nch
    size = half // heads
    group = nch // heads
    share = marks_n // group
    sib = (y, s + 1 - 2 * core)
    xpeer = (y, s + 2 - 4 * x)
    waits = []

    def remote(src, dst, send, recv, device):
        return pltpu.make_async_remote_copy(
            src_ref=src, dst_ref=dst, send_sem=send, recv_sem=recv,
            device_id=device, device_id_type=MESH,
        )

    def chip_dev(offset):
        return (y, lax.rem(chip + offset, nch) * 2 + core)

    def head_dev(offset):
        return (lax.rem(y + offset, n_head), s)

    barrier = pltpu.get_barrier_semaphore()
    peers = [sib] + [head_dev(i) for i in range(1, n_head)] + [chip_dev(i) for i in range(1, nch)]
    for peer in peers:
        pl.semaphore_signal(barrier, inc=1, device_id=peer, device_id_type=MESH)
    pl.semaphore_wait(barrier, len(peers))

    def my_rows(seq_index):
        return pl.ds(pl.multiple_of(seq_index * rows, rows), rows)

    def half_cols(which):
        return pl.ds(pl.multiple_of(which * half, half), half)

    wsib, wloc = [], []
    for p in range(3):
        copy = remote(
            w_ref.at[p, :, half_cols(1 - core)], wg.at[p, my_rows(s), :], wsib_sem.at[0, p],
            wsib_sem.at[1, p], sib,
        )
        copy.start()
        wsib.append(copy)
        copy = pltpu.make_async_copy(
            w_ref.at[p, :, half_cols(core)], wg.at[p, my_rows(s), :], loc_sem.at[p]
        )
        copy.start()
        wloc.append(copy)
    chunk = toks // CHUNKS

    def tok_block(owner, part_index, which_core=None):
        which = core if which_core is None else which_core
        return tokf.at[
            pl.ds(pl.multiple_of(which * toks + part_index * chunk, chunk), chunk),
            pl.ds(pl.multiple_of(owner * feats, feats), feats),
        ]

    def tok_own(part_index):
        return tok_ref.at[pl.ds(part_index * chunk, chunk), :]

    for k in range(CHUNKS):
        for i in range(1, n_head):
            copy = remote(
                tok_own(k), tok_block(y, k), ty_send.at[i, k], ty_recv.at[i, k], head_dev(i)
            )
            copy.start()
            waits.append((None, copy))
    tloc = pltpu.make_async_copy(
        tok_ref,
        tokf.at[
            pl.ds(pl.multiple_of(core * toks, toks), toks),
            pl.ds(pl.multiple_of(y * feats, feats), feats),
        ],
        loc_sem.at[3],
    )
    tloc.start()
    def block(phase, zb, xb):
        at = pl.multiple_of((zb * 2 + xb) * 2 * rows, 2 * rows)
        return wg.at[phase, pl.ds(at, 2 * rows), :]

    def guarded(condition, copy_of):
        @pl.when(condition)
        def _():
            copy_of().start()

        waits.append((condition, copy_of))

    def up(phase, t):
        def copy():
            ref = block(phase, z - t, x)
            return remote(ref, ref, up_send.at[phase, t], up_recv.at[phase, t], (y, s + 4))

        return copy

    def down(phase, t):
        def copy():
            ref = block(phase, z + t, x)
            return remote(ref, ref, dn_send.at[phase, t], dn_recv.at[phase, t], (y, s - 4))

        return copy

    def across(phase, zb):
        def copy():
            ref = block(phase, zb, x)
            return remote(ref, ref, x_send.at[phase, zb], x_recv.at[phase, zb], xpeer)

        return copy

    def from_below(phase, t):
        ref = block(phase, z - 1 - t, x)
        return remote(ref, ref, up_send.at[phase, t], up_recv.at[phase, t], (y, s - 4))

    def from_above(phase, t):
        ref = block(phase, z + 1 + t, x)
        return remote(ref, ref, dn_send.at[phase, t], dn_recv.at[phase, t], (y, s + 4))

    def line_start(phase):
        wloc[phase].wait()
        wsib[phase].wait()
        guarded(z + 1 < nz, up(phase, 0))
        guarded(z >= 1, down(phase, 0))
        copy = across(phase, z)()
        copy.start()
        waits.append((None, copy))

    def line_step(phase, t):
        below = z - 1 - t >= 0
        above = z + 1 + t < nz

        @pl.when(below)
        def _():
            from_below(phase, t).wait_recv()

        if t + 1 < nz - 1:
            guarded(below & (z + 1 < nz), up(phase, t + 1))
        if phase < 2 or t > 0:
            guarded(below, across(phase, z - 1 - t))

        @pl.when(above)
        def _():
            from_above(phase, t).wait_recv()

        if t + 1 < nz - 1:
            guarded(above & (z >= 1), down(phase, t + 1))
        if phase < 2 or t > 0:
            guarded(above, across(phase, z + 1 + t))

    def across_wait(phase, zb):
        ref = block(phase, zb, 1 - x)
        remote(ref, ref, x_send.at[phase, zb], x_recv.at[phase, zb], xpeer).wait_recv()

    def forward_tokens(k):
        for i in range(1, n_head):
            owner = lax.rem(y + n_head - i, n_head)
            ref = tok_block(owner, k)
            remote(ref, ref, ty_send.at[i, k], ty_recv.at[i, k], head_dev(n_head - i)).wait_recv()
            copy = remote(ref, ref, ts_send.at[i, k], ts_recv.at[i, k], sib)
            copy.start()
            waits.append((None, copy))

    line_start(0)
    line_start(1)
    for k in range(CHUNKS):
        copy = remote(tok_own(k), tok_block(y, k), ts_send.at[0, k], ts_recv.at[0, k], sib)
        copy.start()
        waits.append((None, copy))
    for t in range(nz - 1):
        line_step(0, t)
        line_step(1, t)
    line_start(2)
    for k in range(CHUNKS):
        forward_tokens(k)
    tloc.wait()
    for i in range(n_head):
        owner = lax.rem(y + n_head - i, n_head)
        for k in range(CHUNKS):
            ref = tok_block(owner, k, 1 - core)
            remote(ref, ref, ts_send.at[i, k], ts_recv.at[i, k], sib).wait_recv()

    order = [jnp.where(z < nz // 2, i, nz - 1 - i) for i in range(nz)]
    near, far = order[: nz - nz // 4], order[nz - nz // 4 :]
    deep = 4 * rows

    def project(p, blocks, last):
        def body(i, carry):
            at = pl.ds(pl.multiple_of(i * TILE, TILE), TILE)
            total = None
            for zb in blocks:
                inner = pl.ds(pl.multiple_of(zb * deep, deep), deep)
                term = jnp.dot(tokf[at, inner], wg[p, inner, :], preferred_element_type=F32)
                total = term if total is None else total + term
            if last:
                qkv[p, at, :] = (acc[p, at, :] + total).astype(BF)
            else:
                acc[p, at, :] = total
            return carry

        lax.fori_loop(0, 2 * toks // TILE, body, 0)

    def neighbour(step, plane):
        ref = block(2, plane, 1 - x)
        way = (step + 1) // 2
        return remote(ref, ref, near_send.at[way], near_recv.at[way], (y, s + 4 * step))

    def values_wait(zb):
        pl.when(zb == z - 1)(lambda: neighbour(1, z - 1).wait_recv())
        pl.when(zb == z + 1)(lambda: neighbour(-1, z + 1).wait_recv())
        pl.when((zb < z - 1) | (zb > z + 1))(lambda: across_wait(2, zb))

    for zb in near:
        across_wait(0, zb)
    project(0, near, False)
    line_step(2, 0)
    for zb in near:
        across_wait(1, zb)
    project(1, near, False)
    for t in range(1, nz - 1):
        line_step(2, t)
    for zb in far:
        across_wait(0, zb)
    project(0, far, True)
    for zb in far:
        across_wait(1, zb)
    project(1, far, True)

    def cols(h):
        return pl.ds(h * size, size)

    places = lax.broadcasted_iota(jnp.int32, (per_chip, 2 * toks), 1)
    even = lax.broadcasted_iota(jnp.int32, (per_chip, size), 0) % 2 == 0
    own_mark = lax.broadcasted_iota(jnp.int32, (per_chip, marks_n), 1) == (
        chip * per_chip + lax.broadcasted_iota(jnp.int32, (per_chip, marks_n), 0)
    )
    first = chip * (2 * toks)
    for h in range(heads):
        head_pos = pos_ref[pl.ds(core * heads + h, 1), :]
        place = jnp.sum(jnp.where(own_mark, head_pos, 0), -1, keepdims=True) - first
        picker = jnp.where(places == place, 1.0, 0.0).astype(BF)
        picked_q = jnp.dot(picker, qkv[0, :, cols(h)], preferred_element_type=F32)
        picked_k = jnp.dot(picker, qkv[1, :, cols(h)], preferred_element_type=F32)
        marks[chip, h] = jnp.where(even, picked_q, picked_k).astype(BF)

    def all_chips(source, buffer, send, recv):
        for i in range(1, nch):
            copy = remote(source(i), buffer, send.at[i], recv.at[i], chip_dev(i))
            copy.start()
            waits.append((None, copy))

    def from_chips(buffer, send, recv):
        for i in range(1, nch):
            ref = buffer.at[lax.rem(chip + nch - i, nch)]
            remote(ref, ref, send.at[i], recv.at[i], chip_dev(nch - i)).wait_recv()

    all_chips(lambda i: marks.at[chip], marks.at[chip], lm_send, lm_recv)
    across_wait(2, z)
    guarded(z + 1 < nz, lambda: neighbour(1, z))
    guarded(z >= 1, lambda: neighbour(-1, z))
    for zb in near:
        values_wait(zb)
    project(2, near, False)
    from_chips(marks, lm_send, lm_recv)

    def marks_of(h):
        return marks[:, h].astype(F32).reshape(marks_n, size).astype(BF)

    for h in range(heads):
        own = marks_of(h)

        def weigh(i, carry):
            at = pl.ds(pl.multiple_of(i * TILE, TILE), TILE)
            kw[h, :, at] = gauss(own, qkv[1, at, cols(h)]).astype(BF)
            return carry

        lax.fori_loop(0, 2 * toks // TILE, weigh, 0)

    for zb in far:
        values_wait(zb)
    project(2, far, True)

    for h in range(heads):
        total = jnp.dot(kw[h], qkv[2, :, cols(h)], preferred_element_type=F32)
        for j in range(group):
            part[h * group + j] = total[j * share : (j + 1) * share]
    all_chips(
        lambda i: part.at[lax.rem(chip + i, nch)], parts_in.at[chip], rs_send, rs_recv
    )
    mine = marks_of(chip // group)
    inner = gauss(mine, mine)
    scale_cols = jnp.max(jnp.sum(jnp.abs(inner), 0, keepdims=True))
    scale_rows = jnp.max(jnp.sum(jnp.abs(inner), 1, keepdims=True))
    iterate = inner / (scale_cols * scale_rows)
    for step in range(NSTEPS):
        iterate = 2.0 * iterate - exact(exact(iterate, inner), iterate)
    inv[...] = iterate

    for h in range(heads):
        own = marks_of(h)

        def weigh_q(i, carry):
            at = pl.ds(pl.multiple_of(i * TILE, TILE), TILE)
            qw[h, at, :] = gauss(qkv[0, at, cols(h)], own).astype(BF)
            return carry

        lax.fori_loop(0, 2 * toks // TILE, weigh_q, 0)
    from_chips(parts_in, rs_send, rs_recv)
    total = part[chip]
    for i in range(1, nch):
        total = total + parts_in[lax.rem(chip + i, nch)]
    member = lax.rem(chip, group)
    base = chip - member
    summ[member] = total

    def mate(i):
        return lax.rem(member + i, group)

    for i in range(1, group):
        ref = summ.at[member]
        copy = remote(ref, ref, ex_send.at[i], ex_recv.at[i], (y, (base + mate(i)) * 2 + core))
        copy.start()
        waits.append((None, copy))
    for i in range(1, group):
        source = mate(group - i)
        ref = summ.at[source]
        remote(ref, ref, ex_send.at[i], ex_recv.at[i], (y, (base + source) * 2 + core)).wait_recv()
    owned = chip // group
    mixed[owned] = exact(inv[...], summ[...].reshape(marks_n, size)).astype(BF)

    def like(offset):
        return (y, (lax.rem(owned + offset, heads) * group + member) * 2 + core)

    for i in range(1, heads):
        ref = mixed.at[owned]
        copy = remote(ref, ref, ag_send.at[i], ag_recv.at[i], like(i))
        copy.start()
        waits.append((None, copy))
    for i in range(1, heads):
        ref = mixed.at[lax.rem(owned + heads - i, heads)]
        remote(ref, ref, ag_send.at[i], ag_recv.at[i], like(heads - i)).wait_recv()

    own_at = pl.ds(pl.multiple_of(core * toks, toks), toks)
    sib_at = pl.ds(pl.multiple_of((1 - core) * toks, toks), toks)
    for h in range(heads):
        obuf[h] = jnp.dot(qw[h, sib_at, :], mixed[h], preferred_element_type=F32).astype(BF)
        where = pl.ds(pl.multiple_of(core * half + h * size, size), size)
        copy = remote(obuf.at[h], out_ref.at[:, where], os_send.at[h], os_recv.at[h], sib)
        copy.start()
        waits.append((None, copy))
    for h in range(heads):
        where = pl.ds(pl.multiple_of(core * half + h * size, size), size)
        out_ref[:, where] = jnp.dot(
            qw[h, own_at, :], mixed[h], preferred_element_type=F32
        ).astype(BF)
    for h in range(heads):
        where = pl.ds(pl.multiple_of((1 - core) * half + h * size, size), size)
        remote(obuf.at[h], out_ref.at[:, where], os_send.at[h], os_recv.at[h], sib).wait_recv()

    for condition, copy in waits:
        if condition is None:
            copy.wait_send()
        else:
            pl.when(condition)(lambda: copy().wait_send())


def shards(tokens, weights, landmark_pos, n_head, n_seq):
    toks, feats = tokens.shape
    _, rows, wide = weights.shape
    heads = landmark_pos.shape[0] // 2
    marks_n = landmark_pos.shape[1]
    half = wide // 2
    size = half // heads
    nch, nz = n_seq // 2, n_seq // 4
    per_chip = marks_n // nch
    group = nch // heads
    share = marks_n // group
    dma = pltpu.SemaphoreType.DMA
    vmem = pl.BlockSpec(memory_space=pltpu.VMEM)
    return pl.pallas_call(
        functools.partial(kernel, n_head, n_seq),
        out_shape=jax.ShapeDtypeStruct((toks, wide), BF),
        in_specs=[vmem] * 3,
        out_specs=vmem,
        scratch_shapes=[
            pltpu.VMEM((2 * toks, n_head * feats), BF),
            pltpu.VMEM((3, n_seq * rows, half), BF),
            pltpu.VMEM((3, 2 * toks, half), F32),
            pltpu.VMEM((3, 2 * toks, half), BF),
            pltpu.VMEM((nch, heads, per_chip, size), BF),
            pltpu.VMEM((heads, marks_n, 2 * toks), BF),
            pltpu.VMEM((heads, 2 * toks, marks_n), BF),
            pltpu.VMEM((nch, share, size), F32),
            pltpu.VMEM((nch, share, size), F32),
            pltpu.VMEM((group, share, size), F32),
            pltpu.VMEM((marks_n, marks_n), F32),
            pltpu.VMEM((heads, marks_n, size), BF),
            pltpu.VMEM((heads, toks, size), BF),
            dma((4,)), dma((2, 3)),
            dma((n_head, CHUNKS)), dma((n_head, CHUNKS)),
            dma((n_head, CHUNKS)), dma((n_head, CHUNKS)),
            dma((3, nz - 1)), dma((3, nz - 1)), dma((3, nz - 1)), dma((3, nz - 1)),
            dma((3, nz)), dma((3, nz)), dma((2,)), dma((2,)),
            dma((nch,)), dma((nch,)), dma((nch,)), dma((nch,)),
            dma((group,)), dma((group,)), dma((heads,)), dma((heads,)),
            dma((heads,)), dma((heads,)),
        ],
        compiler_params=pltpu.CompilerParams(
            collective_id=0, has_side_effects=True, vmem_limit_bytes=56 * 2**20
        ),
    )(tokens, weights, landmark_pos)


def solution(mesh):
    return jax.shard_map(
        functools.partial(shards, n_head=mesh.shape["head"], n_seq=mesh.shape["seq"]),
        mesh=mesh,
        in_specs=(P("seq", "head"), P(None, "seq", "head"), P("head", None)),
        out_specs=P("seq", "head"),
        check_vma=False,
    )
```

```python
import functools
import math

import jax
import jax.numpy as jnp
from jax import lax
from jax.experimental import pallas as pl
from jax.experimental.pallas import tpu as pltpu
from jax.sharding import PartitionSpec as P

NSTEPS = 6
TILE = 256
CHUNKS = 3
MESH = pl.DeviceIdType.MESH
BF = jnp.bfloat16
F32 = jnp.float32
NT = (((1,), (1,)), ((), ()))


def exact(left, right):
    return jnp.dot(left, right, precision=lax.Precision.HIGHEST, preferred_element_type=F32)


def row_norms(rows):
    wide = rows.astype(F32)
    square = wide * wide
    high = square.astype(BF)
    low = (square - high.astype(F32)).astype(BF)
    ones = jnp.ones((16, rows.shape[1]), BF)
    both = lax.dot_general(ones, high, NT, preferred_element_type=F32) + lax.dot_general(
        ones, low, NT, preferred_element_type=F32
    )
    return both[0:1, :]


def col_norms(rows):
    wide = rows.astype(F32)
    return jnp.sum(wide * wide, -1, keepdims=True)


def gauss(left, right):
    inner = lax.dot_general(left, right, NT, preferred_element_type=F32)
    scale = 1.0 / (2.0 * math.sqrt(left.shape[1]))
    return jnp.exp((2.0 * inner - col_norms(left) - row_norms(right)) * scale)


def kernel(
    n_head, n_seq,
    tok_ref, w_ref, pos_ref, out_ref,
    tokf, wg, acc, qkv, marks, kw, qw, part, parts_in, own_part, summ, inv, mixed, obuf,
    loc_sem, wsib_sem, ty_send, ty_recv, ts_send, ts_recv,
    up_send, up_recv, dn_send, dn_recv, x_send, x_recv, near_send, near_recv,
    lm_send, lm_recv, rs_send, rs_recv, ex_send, ex_recv, ag_send, ag_recv,
    os_send, os_recv,
):
    y = lax.axis_index("head")
    s = lax.axis_index("seq")
    core = lax.rem(s, 2)
    chip = s // 2
    x = lax.rem(chip, 2)
    z = s // 4
    nz = n_seq // 4
    nch = n_seq // 2
    toks, feats = tok_ref.shape
    rows, half = w_ref.shape[1], w_ref.shape[2] // 2
    heads, marks_n = pos_ref.shape[0] // 2, pos_ref.shape[1]
    per_chip = marks_n // nch
    size = half // heads
    group = nch // heads
    share = marks_n // group
    sib = (y, s + 1 - 2 * core)
    xpeer = (y, s + 2 - 4 * x)
    waits = []

    def remote(src, dst, send, recv, device):
        return pltpu.make_async_remote_copy(
            src_ref=src, dst_ref=dst, send_sem=send, recv_sem=recv,
            device_id=device, device_id_type=MESH,
        )

    def chip_dev(offset):
        return (y, lax.rem(chip + offset, nch) * 2 + core)

    def head_dev(offset):
        return (lax.rem(y + offset, n_head), s)

    barrier = pltpu.get_barrier_semaphore()
    peers = [sib] + [head_dev(i) for i in range(1, n_head)] + [chip_dev(i) for i in range(1, nch)]
    for peer in peers:
        pl.semaphore_signal(barrier, inc=1, device_id=peer, device_id_type=MESH)
    pl.semaphore_wait(barrier, len(peers))

    def my_rows(seq_index):
        return pl.ds(pl.multiple_of(seq_index * rows, rows), rows)

    def half_cols(which):
        return pl.ds(pl.multiple_of(which * half, half), half)

    wsib, wloc = [], []
    for p in range(3):
        copy = remote(
            w_ref.at[p, :, half_cols(1 - core)], wg.at[p, my_rows(s), :], wsib_sem.at[0, p],
            wsib_sem.at[1, p], sib,
        )
        copy.start()
        wsib.append(copy)
        copy = pltpu.make_async_copy(
            w_ref.at[p, :, half_cols(core)], wg.at[p, my_rows(s), :], loc_sem.at[p]
        )
        copy.start()
        wloc.append(copy)
    chunk = toks // CHUNKS

    def tok_block(owner, part_index, which_core=None):
        which = core if which_core is None else which_core
        return tokf.at[
            pl.ds(pl.multiple_of(which * toks + part_index * chunk, chunk), chunk),
            pl.ds(pl.multiple_of(owner * feats, feats), feats),
        ]

    def tok_own(part_index):
        return tok_ref.at[pl.ds(part_index * chunk, chunk), :]

    for k in range(CHUNKS):
        for i in range(1, n_head):
            copy = remote(
                tok_own(k), tok_block(y, k), ty_send.at[i, k], ty_recv.at[i, k], head_dev(i)
            )
            copy.start()
            waits.append((None, copy))
    tloc = pltpu.make_async_copy(
        tok_ref,
        tokf.at[
            pl.ds(pl.multiple_of(core * toks, toks), toks),
            pl.ds(pl.multiple_of(y * feats, feats), feats),
        ],
        loc_sem.at[3],
    )
    tloc.start()
    def block(phase, zb, xb):
        at = pl.multiple_of((zb * 2 + xb) * 2 * rows, 2 * rows)
        return wg.at[phase, pl.ds(at, 2 * rows), :]

    def guarded(condition, copy_of):
        @pl.when(condition)
        def _():
            copy_of().start()

        waits.append((condition, copy_of))

    def up(phase, t):
        def copy():
            ref = block(phase, z - t, x)
            return remote(ref, ref, up_send.at[phase, t], up_recv.at[phase, t], (y, s + 4))

        return copy

    def down(phase, t):
        def copy():
            ref = block(phase, z + t, x)
            return remote(ref, ref, dn_send.at[phase, t], dn_recv.at[phase, t], (y, s - 4))

        return copy

    def across(phase, zb):
        def copy():
            ref = block(phase, zb, x)
            return remote(ref, ref, x_send.at[phase, zb], x_recv.at[phase, zb], xpeer)

        return copy

    def from_below(phase, t):
        ref = block(phase, z - 1 - t, x)
        return remote(ref, ref, up_send.at[phase, t], up_recv.at[phase, t], (y, s - 4))

    def from_above(phase, t):
        ref = block(phase, z + 1 + t, x)
        return remote(ref, ref, dn_send.at[phase, t], dn_recv.at[phase, t], (y, s + 4))

    def line_start(phase):
        wloc[phase].wait()
        wsib[phase].wait()
        guarded(z + 1 < nz, up(phase, 0))
        guarded(z >= 1, down(phase, 0))
        copy = across(phase, z)()
        copy.start()
        waits.append((None, copy))

    def line_step(phase, t):
        below = z - 1 - t >= 0
        above = z + 1 + t < nz

        @pl.when(below)
        def _():
            from_below(phase, t).wait_recv()

        if t + 1 < nz - 1:
            guarded(below & (z + 1 < nz), up(phase, t + 1))
        if phase < 2 or t > 0:
            guarded(below, across(phase, z - 1 - t))

        @pl.when(above)
        def _():
            from_above(phase, t).wait_recv()

        if t + 1 < nz - 1:
            guarded(above & (z >= 1), down(phase, t + 1))
        if phase < 2 or t > 0:
            guarded(above, across(phase, z + 1 + t))

    def across_wait(phase, zb):
        ref = block(phase, zb, 1 - x)
        remote(ref, ref, x_send.at[phase, zb], x_recv.at[phase, zb], xpeer).wait_recv()

    def forward_tokens(k):
        for i in range(1, n_head):
            owner = lax.rem(y + n_head - i, n_head)
            ref = tok_block(owner, k)
            remote(ref, ref, ty_send.at[i, k], ty_recv.at[i, k], head_dev(n_head - i)).wait_recv()
            copy = remote(ref, ref, ts_send.at[i, k], ts_recv.at[i, k], sib)
            copy.start()
            waits.append((None, copy))

    line_start(0)
    line_start(1)
    for k in range(CHUNKS):
        copy = remote(tok_own(k), tok_block(y, k), ts_send.at[0, k], ts_recv.at[0, k], sib)
        copy.start()
        waits.append((None, copy))
    for t in range(nz - 1):
        line_step(0, t)
        line_step(1, t)
    line_start(2)
    for k in range(CHUNKS):
        forward_tokens(k)
    tloc.wait()
    for i in range(n_head):
        owner = lax.rem(y + n_head - i, n_head)
        for k in range(CHUNKS):
            ref = tok_block(owner, k, 1 - core)
            remote(ref, ref, ts_send.at[i, k], ts_recv.at[i, k], sib).wait_recv()

    order = [jnp.where(z < nz // 2, i, nz - 1 - i) for i in range(nz)]
    near, far = order[: nz - nz // 4], order[nz - nz // 4 :]
    deep = 4 * rows

    def project(p, blocks, last):
        def body(i, carry):
            at = pl.ds(pl.multiple_of(i * TILE, TILE), TILE)
            total = None
            for zb in blocks:
                inner = pl.ds(pl.multiple_of(zb * deep, deep), deep)
                term = jnp.dot(tokf[at, inner], wg[p, inner, :], preferred_element_type=F32)
                total = term if total is None else total + term
            if last:
                qkv[p, at, :] = (acc[p, at, :] + total).astype(BF)
            else:
                acc[p, at, :] = total
            return carry

        lax.fori_loop(0, 2 * toks // TILE, body, 0)

    def neighbour(step, plane):
        ref = block(2, plane, 1 - x)
        way = (step + 1) // 2
        return remote(ref, ref, near_send.at[way], near_recv.at[way], (y, s + 4 * step))

    def values_wait(zb):
        pl.when(zb == z - 1)(lambda: neighbour(1, z - 1).wait_recv())
        pl.when(zb == z + 1)(lambda: neighbour(-1, z + 1).wait_recv())
        pl.when((zb < z - 1) | (zb > z + 1))(lambda: across_wait(2, zb))

    for zb in near:
        across_wait(0, zb)
    project(0, near, False)
    line_step(2, 0)
    for zb in near:
        across_wait(1, zb)
    project(1, near, False)
    for t in range(1, nz - 1):
        line_step(2, t)
    for zb in far:
        across_wait(0, zb)
    project(0, far, True)
    for zb in far:
        across_wait(1, zb)
    project(1, far, True)

    def cols(h):
        return pl.ds(h * size, size)

    places = lax.broadcasted_iota(jnp.int32, (per_chip, 2 * toks), 1)
    even = lax.broadcasted_iota(jnp.int32, (per_chip, size), 0) % 2 == 0
    own_mark = lax.broadcasted_iota(jnp.int32, (per_chip, marks_n), 1) == (
        chip * per_chip + lax.broadcasted_iota(jnp.int32, (per_chip, marks_n), 0)
    )
    first = chip * (2 * toks)
    for h in range(heads):
        head_pos = pos_ref[pl.ds(core * heads + h, 1), :]
        place = jnp.sum(jnp.where(own_mark, head_pos, 0), -1, keepdims=True) - first
        picker = jnp.where(places == place, 1.0, 0.0).astype(BF)
        picked_q = jnp.dot(picker, qkv[0, :, cols(h)], preferred_element_type=F32)
        picked_k = jnp.dot(picker, qkv[1, :, cols(h)], preferred_element_type=F32)
        marks[chip, h] = jnp.where(even, picked_q, picked_k).astype(BF)

    def all_chips(source, buffer, send, recv):
        for i in range(1, nch):
            copy = remote(source(i), buffer, send.at[i], recv.at[i], chip_dev(i))
            copy.start()
            waits.append((None, copy))

    def from_chips(buffer, send, recv):
        for i in range(1, nch):
            ref = buffer.at[lax.rem(chip + nch - i, nch)]
            remote(ref, ref, send.at[i], recv.at[i], chip_dev(nch - i)).wait_recv()

    all_chips(lambda i: marks.at[chip], marks.at[chip], lm_send, lm_recv)
    across_wait(2, z)
    guarded(z + 1 < nz, lambda: neighbour(1, z))
    guarded(z >= 1, lambda: neighbour(-1, z))
    for zb in near:
        values_wait(zb)
    project(2, near, False)
    from_chips(marks, lm_send, lm_recv)

    def marks_of(h):
        return marks[:, h].astype(F32).reshape(marks_n, size).astype(BF)

    for h in range(heads):
        own = marks_of(h)

        def weigh(i, carry):
            at = pl.ds(pl.multiple_of(i * TILE, TILE), TILE)
            kw[h, :, at] = gauss(own, qkv[1, at, cols(h)]).astype(BF)
            return carry

        lax.fori_loop(0, 2 * toks // TILE, weigh, 0)

    mine = marks_of(chip // group)
    inner = gauss(mine, mine)
    scale_cols = jnp.max(jnp.sum(jnp.abs(inner), 0, keepdims=True))
    scale_rows = jnp.max(jnp.sum(jnp.abs(inner), 1, keepdims=True))
    iterate = inner / (scale_cols * scale_rows)
    for step in range(NSTEPS):
        iterate = 2.0 * iterate - exact(exact(iterate, inner), iterate)
    inv[...] = iterate

    for zb in far:
        values_wait(zb)
    project(2, far, True)

    def share_out(target):
        return remote(
            part.at[target], parts_in.at[chip], rs_send.at[target], rs_recv.at[chip],
            (y, target * 2 + core),
        )

    for h in range(heads):
        total = jnp.dot(kw[h], qkv[2, :, cols(h)], preferred_element_type=F32)
        for j in range(group):
            target = h * group + j
            piece = total[j * share : (j + 1) * share]

            @pl.when(target == chip)
            def _():
                own_part[...] = piece

            part[target] = piece.astype(BF)
            guarded(target != chip, lambda target=target: share_out(target))

    for h in range(heads):
        own = marks_of(h)

        def weigh_q(i, carry):
            at = pl.ds(pl.multiple_of(i * TILE, TILE), TILE)
            qw[h, at, :] = gauss(qkv[0, at, cols(h)], own).astype(BF)
            return carry

        lax.fori_loop(0, 2 * toks // TILE, weigh_q, 0)
    for i in range(1, nch):
        source = lax.rem(chip + i, nch)
        ref = parts_in.at[source]
        remote(ref, ref, rs_send.at[source], rs_recv.at[source], chip_dev(i)).wait_recv()
    total = own_part[...]
    for i in range(1, nch):
        total = total + parts_in[lax.rem(chip + i, nch)].astype(F32)
    member = lax.rem(chip, group)
    base = chip - member
    summ[member] = total

    def mate(i):
        return lax.rem(member + i, group)

    for i in range(1, group):
        ref = summ.at[member]
        copy = remote(ref, ref, ex_send.at[i], ex_recv.at[i], (y, (base + mate(i)) * 2 + core))
        copy.start()
        waits.append((None, copy))
    for i in range(1, group):
        source = mate(group - i)
        ref = summ.at[source]
        remote(ref, ref, ex_send.at[i], ex_recv.at[i], (y, (base + source) * 2 + core)).wait_recv()
    owned = chip // group
    mixed[owned] = exact(inv[...], summ[...].reshape(marks_n, size)).astype(BF)

    def like(offset):
        return (y, (lax.rem(owned + offset, heads) * group + member) * 2 + core)

    for i in range(1, heads):
        ref = mixed.at[owned]
        copy = remote(ref, ref, ag_send.at[i], ag_recv.at[i], like(i))
        copy.start()
        waits.append((None, copy))
    for i in range(1, heads):
        ref = mixed.at[lax.rem(owned + heads - i, heads)]
        remote(ref, ref, ag_send.at[i], ag_recv.at[i], like(heads - i)).wait_recv()

    own_at = pl.ds(pl.multiple_of(core * toks, toks), toks)
    sib_at = pl.ds(pl.multiple_of((1 - core) * toks, toks), toks)
    for h in range(heads):
        obuf[h] = jnp.dot(qw[h, sib_at, :], mixed[h], preferred_element_type=F32).astype(BF)
        where = pl.ds(pl.multiple_of(core * half + h * size, size), size)
        copy = remote(obuf.at[h], out_ref.at[:, where], os_send.at[h], os_recv.at[h], sib)
        copy.start()
        waits.append((None, copy))
    for h in range(heads):
        where = pl.ds(pl.multiple_of(core * half + h * size, size), size)
        out_ref[:, where] = jnp.dot(
            qw[h, own_at, :], mixed[h], preferred_element_type=F32
        ).astype(BF)
    for h in range(heads):
        where = pl.ds(pl.multiple_of((1 - core) * half + h * size, size), size)
        remote(obuf.at[h], out_ref.at[:, where], os_send.at[h], os_recv.at[h], sib).wait_recv()

    for condition, copy in waits:
        if condition is None:
            copy.wait_send()
        else:
            pl.when(condition)(lambda: copy().wait_send())


def shards(tokens, weights, landmark_pos, n_head, n_seq):
    toks, feats = tokens.shape
    _, rows, wide = weights.shape
    heads = landmark_pos.shape[0] // 2
    marks_n = landmark_pos.shape[1]
    half = wide // 2
    size = half // heads
    nch, nz = n_seq // 2, n_seq // 4
    per_chip = marks_n // nch
    group = nch // heads
    share = marks_n // group
    dma = pltpu.SemaphoreType.DMA
    vmem = pl.BlockSpec(memory_space=pltpu.VMEM)
    return pl.pallas_call(
        functools.partial(kernel, n_head, n_seq),
        out_shape=jax.ShapeDtypeStruct((toks, wide), BF),
        in_specs=[vmem] * 3,
        out_specs=vmem,
        scratch_shapes=[
            pltpu.VMEM((2 * toks, n_head * feats), BF),
            pltpu.VMEM((3, n_seq * rows, half), BF),
            pltpu.VMEM((3, 2 * toks, half), F32),
            pltpu.VMEM((3, 2 * toks, half), BF),
            pltpu.VMEM((nch, heads, per_chip, size), BF),
            pltpu.VMEM((heads, marks_n, 2 * toks), BF),
            pltpu.VMEM((heads, 2 * toks, marks_n), BF),
            pltpu.VMEM((nch, share, size), BF),
            pltpu.VMEM((nch, share, size), BF),
            pltpu.VMEM((share, size), F32),
            pltpu.VMEM((group, share, size), F32),
            pltpu.VMEM((marks_n, marks_n), F32),
            pltpu.VMEM((heads, marks_n, size), BF),
            pltpu.VMEM((heads, toks, size), BF),
            dma((4,)), dma((2, 3)),
            dma((n_head, CHUNKS)), dma((n_head, CHUNKS)),
            dma((n_head, CHUNKS)), dma((n_head, CHUNKS)),
            dma((3, nz - 1)), dma((3, nz - 1)), dma((3, nz - 1)), dma((3, nz - 1)),
            dma((3, nz)), dma((3, nz)), dma((2,)), dma((2,)),
            dma((nch,)), dma((nch,)), dma((nch,)), dma((nch,)),
            dma((group,)), dma((group,)), dma((heads,)), dma((heads,)),
            dma((heads,)), dma((heads,)),
        ],
        compiler_params=pltpu.CompilerParams(
            collective_id=0, has_side_effects=True, vmem_limit_bytes=56 * 2**20
        ),
    )(tokens, weights, landmark_pos)


def solution(mesh):
    return jax.shard_map(
        functools.partial(shards, n_head=mesh.shape["head"], n_seq=mesh.shape["seq"]),
        mesh=mesh,
        in_specs=(P("seq", "head"), P(None, "seq", "head"), P("head", None)),
        out_specs=P("seq", "head"),
        check_vma=False,
    )
```

```python
import functools
import math

import jax
import jax.numpy as jnp
from jax import lax
from jax.experimental import pallas as pl
from jax.experimental.pallas import tpu as pltpu
from jax.sharding import PartitionSpec as P

NSTEPS = 6
TILE = 256
CHUNKS = 3
MESH = pl.DeviceIdType.MESH
BF = jnp.bfloat16
F32 = jnp.float32
NT = (((1,), (1,)), ((), ()))


def exact(left, right):
    return jnp.dot(left, right, precision=lax.Precision.HIGHEST, preferred_element_type=F32)


def halves(wide):
    high = wide.astype(BF)
    return high, (wide - high.astype(F32)).astype(BF)


def product(left, right):
    return (
        jnp.dot(left[0], right[1], preferred_element_type=F32)
        + jnp.dot(left[1], right[0], preferred_element_type=F32)
        + jnp.dot(left[0], right[0], preferred_element_type=F32)
    )


def row_norms(rows):
    wide = rows.astype(F32)
    square = wide * wide
    high = square.astype(BF)
    low = (square - high.astype(F32)).astype(BF)
    ones = jnp.ones((16, rows.shape[1]), BF)
    both = lax.dot_general(ones, high, NT, preferred_element_type=F32) + lax.dot_general(
        ones, low, NT, preferred_element_type=F32
    )
    return both[0:1, :]


def col_norms(rows):
    wide = rows.astype(F32)
    return jnp.sum(wide * wide, -1, keepdims=True)


def gauss(left, right):
    inner = lax.dot_general(left, right, NT, preferred_element_type=F32)
    scale = 1.0 / (2.0 * math.sqrt(left.shape[1]))
    return jnp.exp((2.0 * inner - col_norms(left) - row_norms(right)) * scale)


def kernel(
    n_head, n_seq,
    tok_ref, w_ref, pos_ref, out_ref,
    tokf, wg, acc, qkv, marks, kw, qw, part, parts_in, summ, inv, mixed, obuf,
    loc_sem, wsib_sem, ty_send, ty_recv, ts_send, ts_recv,
    up_send, up_recv, dn_send, dn_recv, x_send, x_recv, near_send, near_recv,
    lm_send, lm_recv, rs_send, rs_recv, ex_send, ex_recv, ag_send, ag_recv,
    os_send, os_recv,
):
    y = lax.axis_index("head")
    s = lax.axis_index("seq")
    core = lax.rem(s, 2)
    chip = s // 2
    x = lax.rem(chip, 2)
    z = s // 4
    nz = n_seq // 4
    nch = n_seq // 2
    toks, feats = tok_ref.shape
    rows, half = w_ref.shape[1], w_ref.shape[2] // 2
    heads, marks_n = pos_ref.shape[0] // 2, pos_ref.shape[1]
    per_chip = marks_n // nch
    size = half // heads
    group = nch // heads
    share = marks_n // group
    sib = (y, s + 1 - 2 * core)
    xpeer = (y, s + 2 - 4 * x)
    waits = []

    def remote(src, dst, send, recv, device):
        return pltpu.make_async_remote_copy(
            src_ref=src, dst_ref=dst, send_sem=send, recv_sem=recv,
            device_id=device, device_id_type=MESH,
        )

    def chip_dev(offset):
        return (y, lax.rem(chip + offset, nch) * 2 + core)

    def head_dev(offset):
        return (lax.rem(y + offset, n_head), s)

    barrier = pltpu.get_barrier_semaphore()
    peers = [sib] + [head_dev(i) for i in range(1, n_head)] + [chip_dev(i) for i in range(1, nch)]
    for peer in peers:
        pl.semaphore_signal(barrier, inc=1, device_id=peer, device_id_type=MESH)
    pl.semaphore_wait(barrier, len(peers))

    def my_rows(seq_index):
        return pl.ds(pl.multiple_of(seq_index * rows, rows), rows)

    def half_cols(which):
        return pl.ds(pl.multiple_of(which * half, half), half)

    wsib, wloc = [], []
    for p in range(3):
        copy = remote(
            w_ref.at[p, :, half_cols(1 - core)], wg.at[p, my_rows(s), :], wsib_sem.at[0, p],
            wsib_sem.at[1, p], sib,
        )
        copy.start()
        wsib.append(copy)
        copy = pltpu.make_async_copy(
            w_ref.at[p, :, half_cols(core)], wg.at[p, my_rows(s), :], loc_sem.at[p]
        )
        copy.start()
        wloc.append(copy)
    chunk = toks // CHUNKS

    def tok_block(owner, part_index, which_core=None):
        which = core if which_core is None else which_core
        return tokf.at[
            pl.ds(pl.multiple_of(which * toks + part_index * chunk, chunk), chunk),
            pl.ds(pl.multiple_of(owner * feats, feats), feats),
        ]

    def tok_own(part_index):
        return tok_ref.at[pl.ds(part_index * chunk, chunk), :]

    for k in range(CHUNKS):
        for i in range(1, n_head):
            copy = remote(
                tok_own(k), tok_block(y, k), ty_send.at[i, k], ty_recv.at[i, k], head_dev(i)
            )
            copy.start()
            waits.append((None, copy))
    tloc = pltpu.make_async_copy(
        tok_ref,
        tokf.at[
            pl.ds(pl.multiple_of(core * toks, toks), toks),
            pl.ds(pl.multiple_of(y * feats, feats), feats),
        ],
        loc_sem.at[3],
    )
    tloc.start()
    def block(phase, zb, xb):
        at = pl.multiple_of((zb * 2 + xb) * 2 * rows, 2 * rows)
        return wg.at[phase, pl.ds(at, 2 * rows), :]

    def guarded(condition, copy_of):
        @pl.when(condition)
        def _():
            copy_of().start()

        waits.append((condition, copy_of))

    def up(phase, t):
        def copy():
            ref = block(phase, z - t, x)
            return remote(ref, ref, up_send.at[phase, t], up_recv.at[phase, t], (y, s + 4))

        return copy

    def down(phase, t):
        def copy():
            ref = block(phase, z + t, x)
            return remote(ref, ref, dn_send.at[phase, t], dn_recv.at[phase, t], (y, s - 4))

        return copy

    def across(phase, zb):
        def copy():
            ref = block(phase, zb, x)
            return remote(ref, ref, x_send.at[phase, zb], x_recv.at[phase, zb], xpeer)

        return copy

    def from_below(phase, t):
        ref = block(phase, z - 1 - t, x)
        return remote(ref, ref, up_send.at[phase, t], up_recv.at[phase, t], (y, s - 4))

    def from_above(phase, t):
        ref = block(phase, z + 1 + t, x)
        return remote(ref, ref, dn_send.at[phase, t], dn_recv.at[phase, t], (y, s + 4))

    def line_start(phase):
        wloc[phase].wait()
        wsib[phase].wait()
        guarded(z + 1 < nz, up(phase, 0))
        guarded(z >= 1, down(phase, 0))
        copy = across(phase, z)()
        copy.start()
        waits.append((None, copy))

    def line_step(phase, t):
        below = z - 1 - t >= 0
        above = z + 1 + t < nz

        @pl.when(below)
        def _():
            from_below(phase, t).wait_recv()

        if t + 1 < nz - 1:
            guarded(below & (z + 1 < nz), up(phase, t + 1))
        if phase < 2 or t > 0:
            guarded(below, across(phase, z - 1 - t))

        @pl.when(above)
        def _():
            from_above(phase, t).wait_recv()

        if t + 1 < nz - 1:
            guarded(above & (z >= 1), down(phase, t + 1))
        if phase < 2 or t > 0:
            guarded(above, across(phase, z + 1 + t))

    def across_wait(phase, zb):
        ref = block(phase, zb, 1 - x)
        remote(ref, ref, x_send.at[phase, zb], x_recv.at[phase, zb], xpeer).wait_recv()

    def forward_tokens(k):
        for i in range(1, n_head):
            owner = lax.rem(y + n_head - i, n_head)
            ref = tok_block(owner, k)
            remote(ref, ref, ty_send.at[i, k], ty_recv.at[i, k], head_dev(n_head - i)).wait_recv()
            copy = remote(ref, ref, ts_send.at[i, k], ts_recv.at[i, k], sib)
            copy.start()
            waits.append((None, copy))

    line_start(0)
    line_start(1)
    for k in range(CHUNKS):
        copy = remote(tok_own(k), tok_block(y, k), ts_send.at[0, k], ts_recv.at[0, k], sib)
        copy.start()
        waits.append((None, copy))
    for t in range(nz - 1):
        line_step(0, t)
        line_step(1, t)
    line_start(2)
    for k in range(CHUNKS):
        forward_tokens(k)
    tloc.wait()
    for i in range(n_head):
        owner = lax.rem(y + n_head - i, n_head)
        for k in range(CHUNKS):
            ref = tok_block(owner, k, 1 - core)
            remote(ref, ref, ts_send.at[i, k], ts_recv.at[i, k], sib).wait_recv()

    order = [jnp.where(z < nz // 2, i, nz - 1 - i) for i in range(nz)]
    near, far = order[: nz - nz // 4], order[nz - nz // 4 :]
    deep = 4 * rows

    def project(p, blocks, last):
        def body(i, carry):
            at = pl.ds(pl.multiple_of(i * TILE, TILE), TILE)
            total = None
            for zb in blocks:
                inner = pl.ds(pl.multiple_of(zb * deep, deep), deep)
                term = jnp.dot(tokf[at, inner], wg[p, inner, :], preferred_element_type=F32)
                total = term if total is None else total + term
            if last:
                qkv[p, at, :] = (acc[p, at, :] + total).astype(BF)
            else:
                acc[p, at, :] = total
            return carry

        lax.fori_loop(0, 2 * toks // TILE, body, 0)

    def neighbour(step, plane):
        ref = block(2, plane, 1 - x)
        way = (step + 1) // 2
        return remote(ref, ref, near_send.at[way], near_recv.at[way], (y, s + 4 * step))

    def values_wait(zb):
        pl.when(zb == z - 1)(lambda: neighbour(1, z - 1).wait_recv())
        pl.when(zb == z + 1)(lambda: neighbour(-1, z + 1).wait_recv())
        pl.when((zb < z - 1) | (zb > z + 1))(lambda: across_wait(2, zb))

    for zb in near:
        across_wait(0, zb)
    project(0, near, False)
    line_step(2, 0)
    for zb in near:
        across_wait(1, zb)
    project(1, near, False)
    for t in range(1, nz - 1):
        line_step(2, t)
    for zb in far:
        across_wait(0, zb)
    project(0, far, True)
    for zb in far:
        across_wait(1, zb)
    project(1, far, True)

    def cols(h):
        return pl.ds(h * size, size)

    places = lax.broadcasted_iota(jnp.int32, (per_chip, 2 * toks), 1)
    even = lax.broadcasted_iota(jnp.int32, (per_chip, size), 0) % 2 == 0
    own_mark = lax.broadcasted_iota(jnp.int32, (per_chip, marks_n), 1) == (
        chip * per_chip + lax.broadcasted_iota(jnp.int32, (per_chip, marks_n), 0)
    )
    first = chip * (2 * toks)
    for h in range(heads):
        head_pos = pos_ref[pl.ds(core * heads + h, 1), :]
        place = jnp.sum(jnp.where(own_mark, head_pos, 0), -1, keepdims=True) - first
        picker = jnp.where(places == place, 1.0, 0.0).astype(BF)
        picked_q = jnp.dot(picker, qkv[0, :, cols(h)], preferred_element_type=F32)
        picked_k = jnp.dot(picker, qkv[1, :, cols(h)], preferred_element_type=F32)
        marks[chip, h] = jnp.where(even, picked_q, picked_k).astype(BF)

    def all_chips(source, buffer, send, recv):
        for i in range(1, nch):
            copy = remote(source(i), buffer, send.at[i], recv.at[i], chip_dev(i))
            copy.start()
            waits.append((None, copy))

    def from_chips(buffer, send, recv):
        for i in range(1, nch):
            ref = buffer.at[lax.rem(chip + nch - i, nch)]
            remote(ref, ref, send.at[i], recv.at[i], chip_dev(nch - i)).wait_recv()

    all_chips(lambda i: marks.at[chip], marks.at[chip], lm_send, lm_recv)
    across_wait(2, z)
    guarded(z + 1 < nz, lambda: neighbour(1, z))
    guarded(z >= 1, lambda: neighbour(-1, z))
    for zb in near:
        values_wait(zb)
    project(2, near, False)
    from_chips(marks, lm_send, lm_recv)

    def marks_of(h):
        return marks[:, h].astype(F32).reshape(marks_n, size).astype(BF)

    for h in range(heads):
        own = marks_of(h)

        def weigh(i, carry):
            at = pl.ds(pl.multiple_of(i * TILE, TILE), TILE)
            kw[h, :, at] = gauss(own, qkv[1, at, cols(h)]).astype(BF)
            return carry

        lax.fori_loop(0, 2 * toks // TILE, weigh, 0)

    for zb in far:
        values_wait(zb)
    project(2, far, True)

    def share_out(target):
        return remote(
            part.at[target], parts_in.at[chip], rs_send.at[target], rs_recv.at[chip],
            (y, target * 2 + core),
        )

    for h in range(heads):
        total = jnp.dot(kw[h], qkv[2, :, cols(h)], preferred_element_type=F32)
        for j in range(group):
            target = h * group + j
            part[target] = total[j * share : (j + 1) * share]
            guarded(target != chip, lambda target=target: share_out(target))

    mine = marks_of(chip // group)
    inner = gauss(mine, mine)
    scale_cols = jnp.max(jnp.sum(jnp.abs(inner), 0, keepdims=True))
    scale_rows = jnp.max(jnp.sum(jnp.abs(inner), 1, keepdims=True))
    iterate = inner / (scale_cols * scale_rows)
    inner_halves = halves(inner)
    for step in range(NSTEPS):
        now = halves(iterate)
        left = halves(product(now, inner_halves))
        iterate = 2.0 * iterate - product(left, now)
    inv[...] = iterate

    for h in range(heads):
        own = marks_of(h)

        def weigh_q(i, carry):
            at = pl.ds(pl.multiple_of(i * TILE, TILE), TILE)
            qw[h, at, :] = gauss(qkv[0, at, cols(h)], own).astype(BF)
            return carry

        lax.fori_loop(0, 2 * toks // TILE, weigh_q, 0)
    for i in range(1, nch):
        source = lax.rem(chip + i, nch)
        ref = parts_in.at[source]
        remote(ref, ref, rs_send.at[source], rs_recv.at[source], chip_dev(i)).wait_recv()
    total = part[chip]
    for i in range(1, nch):
        total = total + parts_in[lax.rem(chip + i, nch)]
    member = lax.rem(chip, group)
    base = chip - member
    summ[member] = total

    def mate(i):
        return lax.rem(member + i, group)

    for i in range(1, group):
        ref = summ.at[member]
        copy = remote(ref, ref, ex_send.at[i], ex_recv.at[i], (y, (base + mate(i)) * 2 + core))
        copy.start()
        waits.append((None, copy))
    for i in range(1, group):
        source = mate(group - i)
        ref = summ.at[source]
        remote(ref, ref, ex_send.at[i], ex_recv.at[i], (y, (base + source) * 2 + core)).wait_recv()
    owned = chip // group
    mixed[owned] = exact(inv[...], summ[...].reshape(marks_n, size)).astype(BF)

    def like(offset):
        return (y, (lax.rem(owned + offset, heads) * group + member) * 2 + core)

    for i in range(1, heads):
        ref = mixed.at[owned]
        copy = remote(ref, ref, ag_send.at[i], ag_recv.at[i], like(i))
        copy.start()
        waits.append((None, copy))
    for i in range(1, heads):
        ref = mixed.at[lax.rem(owned + heads - i, heads)]
        remote(ref, ref, ag_send.at[i], ag_recv.at[i], like(heads - i)).wait_recv()

    own_at = pl.ds(pl.multiple_of(core * toks, toks), toks)
    sib_at = pl.ds(pl.multiple_of((1 - core) * toks, toks), toks)
    for h in range(heads):
        obuf[h] = jnp.dot(qw[h, sib_at, :], mixed[h], preferred_element_type=F32).astype(BF)
        where = pl.ds(pl.multiple_of(core * half + h * size, size), size)
        copy = remote(obuf.at[h], out_ref.at[:, where], os_send.at[h], os_recv.at[h], sib)
        copy.start()
        waits.append((None, copy))
    for h in range(heads):
        where = pl.ds(pl.multiple_of(core * half + h * size, size), size)
        out_ref[:, where] = jnp.dot(
            qw[h, own_at, :], mixed[h], preferred_element_type=F32
        ).astype(BF)
    for h in range(heads):
        where = pl.ds(pl.multiple_of((1 - core) * half + h * size, size), size)
        remote(obuf.at[h], out_ref.at[:, where], os_send.at[h], os_recv.at[h], sib).wait_recv()

    for condition, copy in waits:
        if condition is None:
            copy.wait_send()
        else:
            pl.when(condition)(lambda: copy().wait_send())


def shards(tokens, weights, landmark_pos, n_head, n_seq):
    toks, feats = tokens.shape
    _, rows, wide = weights.shape
    heads = landmark_pos.shape[0] // 2
    marks_n = landmark_pos.shape[1]
    half = wide // 2
    size = half // heads
    nch, nz = n_seq // 2, n_seq // 4
    per_chip = marks_n // nch
    group = nch // heads
    share = marks_n // group
    dma = pltpu.SemaphoreType.DMA
    vmem = pl.BlockSpec(memory_space=pltpu.VMEM)
    return pl.pallas_call(
        functools.partial(kernel, n_head, n_seq),
        out_shape=jax.ShapeDtypeStruct((toks, wide), BF),
        in_specs=[vmem] * 3,
        out_specs=vmem,
        scratch_shapes=[
            pltpu.VMEM((2 * toks, n_head * feats), BF),
            pltpu.VMEM((3, n_seq * rows, half), BF),
            pltpu.VMEM((3, 2 * toks, half), F32),
            pltpu.VMEM((3, 2 * toks, half), BF),
            pltpu.VMEM((nch, heads, per_chip, size), BF),
            pltpu.VMEM((heads, marks_n, 2 * toks), BF),
            pltpu.VMEM((heads, 2 * toks, marks_n), BF),
            pltpu.VMEM((nch, share, size), F32),
            pltpu.VMEM((nch, share, size), F32),
            pltpu.VMEM((group, share, size), F32),
            pltpu.VMEM((marks_n, marks_n), F32),
            pltpu.VMEM((heads, marks_n, size), BF),
            pltpu.VMEM((heads, toks, size), BF),
            dma((4,)), dma((2, 3)),
            dma((n_head, CHUNKS)), dma((n_head, CHUNKS)),
            dma((n_head, CHUNKS)), dma((n_head, CHUNKS)),
            dma((3, nz - 1)), dma((3, nz - 1)), dma((3, nz - 1)), dma((3, nz - 1)),
            dma((3, nz)), dma((3, nz)), dma((2,)), dma((2,)),
            dma((nch,)), dma((nch,)), dma((nch,)), dma((nch,)),
            dma((group,)), dma((group,)), dma((heads,)), dma((heads,)),
            dma((heads,)), dma((heads,)),
        ],
        compiler_params=pltpu.CompilerParams(
            collective_id=0, has_side_effects=True, vmem_limit_bytes=56 * 2**20
        ),
    )(tokens, weights, landmark_pos)


def solution(mesh):
    return jax.shard_map(
        functools.partial(shards, n_head=mesh.shape["head"], n_seq=mesh.shape["seq"]),
        mesh=mesh,
        in_specs=(P("seq", "head"), P(None, "seq", "head"), P("head", None)),
        out_specs=P("seq", "head"),
        check_vma=False,
    )
```
